256 devices in a mesh: dp: 8 (over z), expert: 32 (over x, y, core).
Axes of the slice: x: 4, y: 4, z: 8, core: 2. Of those that a mesh axis runs over, the one named last changes fastest.
Arguments:
- tokens: bfloat16 [32768, 3584], P(('dp', 'expert')), may hold values from -6 to 6
- routes: int32 [32768, 2], P(('dp', 'expert')), may hold values from 0 to 31, all different within a row; in each aligned block of 128 rows (0 to 127, 128 to 255, ...) at most 10 rows name the same one
- scores: bfloat16 [32768, 2], P(('dp', 'expert')), may hold values from 0.099609375 to 1
- out_grad: bfloat16 [32768, 3584], P(('dp', 'expert')), may hold values from -0.8984375 to 0.8984375
- w_up: bfloat16 [32, 1024, 3584], P('expert', 'dp'), may hold values from -0.09375 to 0.09375
- w_down: bfloat16 [32, 1024, 3584], P('expert', 'dp'), may hold values from -0.1875 to 0.1875
Outputs:
- grad_tokens: bfloat16 [32768, 3584], P(('dp', 'expert'))
- grad_scores: bfloat16 [32768, 2], P(('dp', 'expert'))
- grad_up: bfloat16 [32, 1024, 3584], P('expert', 'dp')
- grad_down: bfloat16 [32, 1024, 3584], P('expert', 'dp')
The draws below stay inside these ranges and needn't reach their ends.
Inputs may be any that keep to these rules, and one draw needn't show every extreme that they name: `routes`: each row names 2 different experts. Among the 128 rows of one device no expert is named more than 10 times, and in every draw some device names some expert exactly 10 times.
All inputs are finite; a program needn't handle non-finite values.
Results may differ from the reference program's by a relative error of at most 0.017.
Values may be sent and summed in bfloat16 or wider, within the bound.
A program may use at most 192 MiB of HBM per device.

```python
import math
import jax
import jax.numpy as jnp
import numpy as np
from jax import lax

D = 3584
F = 1024
TOK_DEV = 128
EXPERTS = 32
TOPK = 2
CAP = 10
TOKENS = 32768
N_DP = 8
N_EXPERT = 32


def level_of(rng, shape, split, least, largest):
    gain, own = 1.0, jax.random.fold_in(rng, 6)
    for dim, blocks in split:
        heights = jnp.exp(jax.random.uniform(jax.random.fold_in(own, dim), (blocks,), jnp.float32, least / len(split), largest / len(split)))
        gain = gain * jnp.repeat(heights, shape[dim] // blocks).reshape([-1 if axis == dim else 1 for axis in range(len(shape))])
    return gain


def shared_out(rng, own, number, rows, count, top, limit, slope):
    order = jax.random.permutation(rng, count)
    crowded, ordinary = load_shares(count, rows * top, limit, slope, True), load_shares(count, rows * top, limit, slope, False)
    places = jnp.arange(count)

    def named(tallies, rotation):
        used = int((tallies > 0).sum())
        fixed = max(1, used // 4)
        moved = fixed + (places - fixed + rotation * (used - fixed)) % max(1, count - fixed)
        return jnp.zeros((count,), jnp.int32).at[order[jnp.where(places < fixed, places, moved)]].set(jnp.asarray(tallies, jnp.int32))

    tallies = jnp.where(number % 4 == 0, named(crowded, number // 4), named(ordinary, number - number // 4 - 1))
    mixed = jax.random.permutation(jax.random.fold_in(own, 3), count)
    source_of, sink = mixed[0:count // 2 * 2:2], mixed[1:count // 2 * 2:2]
    slack = jnp.minimum(tallies[source_of] - 1, limit - tallies[sink]) // 2
    slack = jnp.where((source_of == order[0]) | (sink == order[0]) | (tallies[sink] == 0), 0, jnp.maximum(slack, 0))
    moved = jax.random.randint(jax.random.fold_in(own, 4), (count // 2,), 0, 1 << 20) % (slack + 1)
    tallies = tallies.at[source_of].add(-moved).at[sink].add(moved)
    members = jnp.searchsorted(jnp.cumsum(tallies), jnp.arange(rows * top), side="right").astype(jnp.int32)
    grid = members.reshape(top, rows).T
    grid = grid[jax.random.permutation(jax.random.fold_in(own, 1), rows)]
    rotation = jax.random.randint(jax.random.fold_in(own, 2), (rows, 1), 0, top)
    return jnp.take_along_axis(grid, (jnp.arange(top)[None, :] + rotation) % top, axis=1)


def load_shares(amount, total, most, slope, full):
    loads = [(1 << 20) // math.isqrt(grade ** slope) + 1 for grade in range(1, amount + 1)]
    largest = most if full else min(most, max(-(-total // amount), total * loads[0] // sum(loads)))
    least = 1 if total - largest >= amount - 1 else 0
    counts, surplus = [largest] + [least] * (amount - 1), total - largest - least * (amount - 1)
    while surplus > 0:
        free = [i for i in range(1, amount) if counts[i] < largest] or [i for i in range(1, amount) if counts[i] < most]
        pool, left = sum([loads[i] for i in free]), surplus
        for i in free:
            addition = min(most - counts[i], max(1, left * loads[i] // pool), surplus)
            counts[i] = counts[i] + addition
            surplus = surplus - addition
    return np.array(counts)


def normal_values(stream_key, shape, deviation, bound, cuts=(), held_as=jnp.bfloat16):
    drawn = deviation * jax.random.normal(stream_key, shape, jnp.float32)
    if cuts:
        drawn = drawn * level_of(stream_key, shape, cuts, -0.22, 0.18)
    return jnp.clip(drawn, -bound, bound).astype(held_as)


def setup_inputs(seed: int = 0) -> dict:
    key_of = jax.random.split(jax.random.key(seed), 7)
    tokens = normal_values(key_of[0], (TOKENS, D), 1.0, 6.0, ((0, 256),))
    routes_keys = jax.random.split(jax.random.fold_in(key_of[1], 1), TOKENS // TOK_DEV)
    routes_turns = jax.random.permutation(jax.random.fold_in(key_of[1], 3), TOKENS // TOK_DEV)
    routes = jax.vmap(lambda own, number: shared_out(jax.random.fold_in(key_of[1], 2), own, number, TOK_DEV, EXPERTS, TOPK, CAP, 2))(routes_keys, routes_turns).reshape((TOKENS, TOPK))
    scores = jnp.clip(0.099609375 + 0.9003906 * jax.random.uniform(key_of[2], (TOKENS, TOPK), jnp.float32) ** level_of(key_of[2], (TOKENS, TOPK), ((0, 256),), -0.2, 0.2), 0.099609375, 1.0).astype(jnp.bfloat16)
    out_grad = normal_values(key_of[3], (TOKENS, D), 0.15, 0.8984375, ((0, 256),))
    w_up = normal_values(key_of[4], (EXPERTS, F, D), D ** -0.5, 0.09375, ((0, 32), (1, 8)))
    w_down = normal_values(key_of[5], (EXPERTS, F, D), F ** -0.5, 0.1875, ((0, 32), (1, 8)))
    return {"tokens": tokens, "routes": routes, "scores": scores, "out_grad": out_grad, "w_up": w_up, "w_down": w_down}


def silu_grad(preact):
    sig = jax.nn.sigmoid(preact)
    return sig * (1.0 + preact * (1.0 - sig))

def reference(tokens, routes, scores, out_grad, w_up, w_down):
    top_k = routes.shape[1]
    per_device = TOK_DEV * top_k
    slot_count = N_EXPERT * CAP
    assigned = TOKENS * top_k
    flat_routes = routes.reshape(assigned)
    onehot = (flat_routes[:, None] == jnp.arange(EXPERTS, dtype=jnp.int32)[None, :]).astype(jnp.int32)
    onehot = onehot.reshape(N_DP * N_EXPERT, per_device, EXPERTS)
    before = jnp.cumsum(onehot, axis=1) - onehot
    order_rank = lax.optimization_barrier(jnp.sum(before * onehot, axis=2)).reshape(assigned).astype(jnp.int32)
    indices = jnp.arange(assigned, dtype=jnp.int32)
    device_of = indices // per_device
    group_of = device_of // N_EXPERT
    slot_of = device_of % N_EXPERT * CAP + order_rank
    token_ext = jnp.concatenate([tokens, jnp.zeros((1, D), jnp.bfloat16)], axis=0)
    grad_ext = jnp.concatenate([out_grad, jnp.zeros((1, D), jnp.bfloat16)], axis=0)
    score_ext = jnp.concatenate([scores.reshape(assigned), jnp.zeros((1,), jnp.bfloat16)], axis=0)

    def per_expert(carry, expert):
        token_acc, score_acc = carry
        up_rows = w_up[expert].astype(jnp.float32)
        down_rows = w_down[expert].astype(jnp.float32)
        group_key = jnp.where(flat_routes == expert, group_of, N_DP).astype(jnp.int32)
        slot_map = jnp.full((N_DP, slot_count), assigned, jnp.int32)
        slot_map = slot_map.at[group_key, slot_of].set(indices, mode='drop')
        token_rows = (slot_map // top_k).astype(jnp.int32)
        inputs = token_ext[token_rows]
        grads = grad_ext[token_rows]
        slot_scores = score_ext[slot_map]
        preact = jnp.einsum('grd,fd->grf', inputs.astype(jnp.float32), up_rows)
        active = jax.nn.silu(preact).astype(jnp.bfloat16)
        output = jnp.einsum('grf,fd->grd', active.astype(jnp.float32), down_rows)
        score_grad = lax.optimization_barrier(jnp.sum(grads.astype(jnp.float32) * output, axis=2)).astype(jnp.bfloat16)
        weighted = (slot_scores.astype(jnp.float32)[:, :, None] * grads.astype(jnp.float32)).astype(jnp.bfloat16)
        hidden_grad = jnp.einsum('grd,fd->grf', weighted.astype(jnp.float32), down_rows)
        pre_grad = (hidden_grad * silu_grad(preact)).astype(jnp.bfloat16)
        token_grad = jnp.einsum('grf,fd->grd', pre_grad.astype(jnp.float32), up_rows).astype(jnp.bfloat16)
        up_parts = jnp.einsum('grf,grd->gfd', pre_grad.astype(jnp.float32), inputs.astype(jnp.float32)).astype(jnp.bfloat16)
        down_parts = jnp.einsum('grf,grd->gfd', active.astype(jnp.float32), weighted.astype(jnp.float32)).astype(jnp.bfloat16)
        up_parts, down_parts = lax.optimization_barrier((up_parts, down_parts))
        grad_up_one = lax.optimization_barrier(jnp.sum(up_parts.astype(jnp.float32), axis=0)).astype(jnp.bfloat16)
        grad_down_one = lax.optimization_barrier(jnp.sum(down_parts.astype(jnp.float32), axis=0)).astype(jnp.bfloat16)
        token_acc = token_acc.at[token_rows.reshape(-1)].add(token_grad.reshape(-1, D).astype(jnp.float32), mode='drop')
        score_acc = score_acc.at[slot_map.reshape(-1)].add(score_grad.reshape(-1).astype(jnp.float32), mode='drop')
        return ((token_acc, score_acc), (grad_up_one, grad_down_one))
    start_state = (jnp.zeros((TOKENS, D), jnp.float32), jnp.zeros((assigned,), jnp.float32))
    final_state, weight_grads = lax.scan(per_expert, start_state, jnp.arange(EXPERTS, dtype=jnp.int32))
    token_acc, score_acc = final_state
    grad_up, grad_down = weight_grads
    grad_tokens = token_acc.astype(jnp.bfloat16)
    grad_scores = score_acc.reshape(TOKENS, top_k).astype(jnp.bfloat16)
    return (grad_tokens, grad_scores, grad_up, grad_down)
```

```python
import functools

import jax
import jax.numpy as jnp
from jax import lax
from jax.experimental import pallas as pl
from jax.experimental.pallas import tpu as pltpu
from jax.sharding import PartitionSpec as P

MESH = pl.DeviceIdType.MESH
BF = jnp.bfloat16
F32 = jnp.float32
ROWS = 16
LANES = 128


def dot_nn(a, b):
    return lax.dot_general(a, b, (((1,), (0,)), ((), ())), preferred_element_type=F32)


def dot_nt(a, b):
    return lax.dot_general(a, b, (((1,), (1,)), ((), ())), preferred_element_type=F32)


def kernel(
    n_dp, n_ex, D, FB, T,
    tok_ref, grad_ref, up_ref, down_ref, routes_ref, scores_ref,
    gtok_ref, gscore_ref, gup_ref, gdown_ref,
    tokv, gradv, send, recv, back, wup, wdn, rs, far, du, dut, ht, sacc, pmat,
    loc_sem, ag_s, ag_r, di_s, di_r, re_s, re_r, rs_s, rs_r, far_s, out_sem,
):
    g = lax.axis_index("dp")
    me = lax.axis_index("expert")
    right, left = lax.rem(g + 1, n_dp), lax.rem(g + n_dp - 1, n_dp)
    S = n_ex * ROWS
    H = D // 2

    loads = [
        pltpu.make_async_copy(tok_ref, tokv, loc_sem.at[0]),
        pltpu.make_async_copy(grad_ref, gradv, loc_sem.at[1]),
        pltpu.make_async_copy(up_ref, wup.at[pl.ds(0, FB)], loc_sem.at[2]),
        pltpu.make_async_copy(down_ref, wdn.at[pl.ds(0, FB)], loc_sem.at[3]),
    ]
    for c in loads:
        c.start()

    barrier = pltpu.get_barrier_semaphore()
    for z in (right, left):
        pl.semaphore_signal(barrier, inc=1, device_id=(z, me), device_id_type=MESH)

    def greet(d, _):
        pl.semaphore_signal(
            barrier, inc=1, device_id=(g, lax.rem(me + d, n_ex)), device_id_type=MESH
        )
        return 0

    lax.fori_loop(1, n_ex, greet, 0)
    pl.semaphore_wait(barrier, n_ex + 1)

    def slot(arm, d):
        return 0 if d == 0 else (7 if d == 4 else 2 * d - 1 + arm)

    def ag(arm, d, m):
        buf, own = (wup, up_ref) if m == 0 else (wdn, down_ref)
        src = own if d == 1 else buf.at[pl.ds(slot(arm, d - 1) * FB, FB)]
        return pltpu.make_async_remote_copy(
            src_ref=src,
            dst_ref=buf.at[pl.ds(slot(arm, d) * FB, FB)],
            send_sem=ag_s.at[arm, d - 1, m],
            recv_sem=ag_r.at[arm, d - 1, m],
            device_id=(right if arm == 0 else left, me),
            device_id_type=MESH,
        )

    def ag_has(arm, d, m):
        return d <= 3 or m == arm

    def order(arm):
        return (0, 1) if arm == 0 else (1, 0)

    for i in range(2):
        for arm in range(2):
            ag(arm, 1, order(arm)[i]).start()

    def ag_step(d):
        for i in range(2):
            for arm in range(2):
                m = order(arm)[i]
                if ag_has(arm, d, m):
                    ag(arm, d, m).wait_recv()
                    if d < 4 and ag_has(arm, d + 1, m):
                        ag(arm, d + 1, m).start()

    lane = lax.broadcasted_iota(jnp.int32, (T, LANES), 1)
    rels, onehots = [], []
    for k in range(2):
        rel = routes_ref[:, k : k + 1] - me
        rel = jnp.where(rel < 0, rel + n_ex, rel)
        rels.append(rel)
        onehots.append((lane == rel).astype(F32))
    tri = (
        lax.broadcasted_iota(jnp.int32, (T, T), 1) < lax.broadcasted_iota(jnp.int32, (T, T), 0)
    ).astype(F32)
    before = dot_nn(tri.astype(BF), (onehots[0] + onehots[1]).astype(BF))
    slots = lax.broadcasted_iota(jnp.int32, (T, S), 1)
    pts = []
    for k in range(2):
        rank = jnp.sum(before * onehots[k], axis=1, keepdims=True).astype(jnp.int32)
        place = (slots == rels[k] * ROWS + rank).astype(F32)
        pmat[k] = place.astype(BF)
        pts.append(place.T.astype(BF))
    pt = pts[0] + pts[1]
    cols = D // 7
    loads[0].wait()
    for j in range(7):
        send[:, j * cols : (j + 1) * cols] = dot_nn(pt, tokv[:, j * cols : (j + 1) * cols]).astype(BF)
    loads[1].wait()
    for j in range(7):
        send[:, D + j * cols : D + (j + 1) * cols] = dot_nn(
            pt, gradv[:, j * cols : (j + 1) * cols]
        ).astype(BF)
    sc = [jnp.broadcast_to(scores_ref[:, k : k + 1], (T, LANES)) for k in range(2)]
    send[:, 2 * D :] = (dot_nn(pts[0], sc[0]) + dot_nn(pts[1], sc[1])).astype(BF)
    recv[0:ROWS, :] = send[0:ROWS, :]

    def block(d):
        return pl.ds(pl.multiple_of(d * ROWS, ROWS), ROWS)

    def dispatch(d):
        return pltpu.make_async_remote_copy(
            src_ref=send.at[block(d)],
            dst_ref=recv.at[block(d)],
            send_sem=di_s.at[d],
            recv_sem=di_r.at[d],
            device_id=(g, lax.rem(me + d, n_ex)),
            device_id_type=MESH,
        )

    def giveback(d):
        return pltpu.make_async_remote_copy(
            src_ref=send.at[block(d), pl.ds(0, D + LANES)],
            dst_ref=back.at[block(d)],
            send_sem=re_s.at[d],
            recv_sem=re_r.at[d],
            device_id=(g, lax.rem(me + n_ex - d, n_ex)),
            device_id_type=MESH,
        )

    def each(action):
        def body(d, _):
            action(d)
            return 0

        lax.fori_loop(1, n_ex, body, 0)

    each(lambda d: dispatch(d).start())
    sacc[...] = jnp.zeros_like(sacc)

    def hidden(first, count):
        n = count * FB
        rows = slice(first * FB, first * FB + n)
        c = recv[:, 2 * D :].astype(F32)
        if count == 2:
            c = jnp.concatenate([c, c], axis=1)
        u = dot_nt(recv[:, :D], wup[rows, :])
        s = dot_nt(recv[:, D : 2 * D], wdn[rows, :])
        sig = jax.nn.sigmoid(u)
        h = (u * sig).astype(BF).astype(F32)
        score = h * s
        for i in range(count):
            sacc[...] += score[:, i * FB : (i + 1) * FB]
        dpre = c * s * (sig * (1.0 + u * (1.0 - sig)))
        du[:, rows] = dpre.astype(BF)
        dut[rows, :] = dpre.T.astype(BF)
        ht[rows, :] = (h * c).T.astype(BF)

    ag_step(1)
    ag_step(2)
    ag_step(3)
    each(lambda d: dispatch(d).wait_recv())
    for c in loads[2:]:
        c.wait()
    hidden(0, 1)
    for d in (1, 2, 3):
        hidden(2 * d - 1, 2)
    ag_step(4)
    hidden(7, 1)

    def term(chunk, m, half):
        lhs = dut if m == 0 else ht
        at = (0 if m == 0 else D) + half * H
        return dot_nn(lhs[chunk * FB : (chunk + 1) * FB, :], recv[:, at : at + H])

    def rs_copy(arm, d, m, half):
        cs = pl.ds(half * H, H)
        src = far.at[arm, :, cs] if d == 4 else rs.at[arm, d, m, :, cs]
        return pltpu.make_async_remote_copy(
            src_ref=src,
            dst_ref=rs.at[arm, d - 1, m, :, cs],
            send_sem=far_s.at[arm, half] if d == 4 else rs_s.at[arm, d, m, half],
            recv_sem=rs_r.at[arm, d - 1, m, half],
            device_id=(left if arm == 0 else right, me),
            device_id_type=MESH,
        )

    def rs_piece(arm, d, m, half):
        cs = slice(half * H, (half + 1) * H)
        t = term(slot(arm, d), m, half)
        if d == 4:
            far[arm, :, cs] = t.astype(BF)
        elif d == 3 and m != arm:
            rs[arm, d, m, :, cs] = t.astype(BF)
        else:
            rs_copy(arm, d + 1, m, half).wait_recv()
            rs[arm, d, m, :, cs] = (t + rs[arm, d, m, :, cs].astype(F32)).astype(BF)
        rs_copy(arm, d, m, half).start()

    for half in range(2):
        for arm in range(2):
            rs_piece(arm, 4, arm, half)
    for half in range(2):
        for arm in range(2):
            rs_piece(arm, 3, 1 - arm, half)

    each(lambda d: dispatch(d).wait_send())
    for j in range(7):
        send[:, j * cols : (j + 1) * cols] = dot_nn(
            du[...], wup[:, j * cols : (j + 1) * cols]
        ).astype(BF)
    total = jnp.sum(sacc[...], axis=1, keepdims=True)
    send[:, D : D + LANES] = jnp.broadcast_to(total, (S, LANES)).astype(BF)
    back[0:ROWS, :] = send[0:ROWS, 0 : D + LANES]
    each(lambda d: giveback(d).start())

    for half in range(2):
        for arm in range(2):
            rs_piece(arm, 3, arm, half)
    for d in (2, 1):
        for i in range(2):
            for half in range(2):
                for arm in range(2):
                    rs_piece(arm, d, (1 - arm) if i == 0 else arm, half)

    each(lambda d: giveback(d).wait_recv())
    both = pmat[0] + pmat[1]
    for j in range(7):
        tokv[:, j * cols : (j + 1) * cols] = dot_nn(both, back[:, j * cols : (j + 1) * cols]).astype(BF)
    outs = [pltpu.make_async_copy(tokv, gtok_ref, out_sem.at[0])]
    outs[0].start()
    tails = [dot_nn(pmat[k], back[:, D:]) for k in range(2)]
    gscore_ref[...] = jnp.where(lane == 0, tails[0], tails[1])[:, 0:2].astype(BF)

    t_out = 1
    for half in range(2):
        for m in range(2):
            cs = slice(half * H, (half + 1) * H)
            t = term(0, m, half)
            for arm in range(2):
                rs_copy(arm, 1, m, half).wait_recv()
                t = t + rs[arm, 0, m, :, cs].astype(F32)
            rs[0, 0, m, :, cs] = t.astype(BF)
            ref = gup_ref if m == 0 else gdown_ref
            o = pltpu.make_async_copy(
                rs.at[0, 0, m, :, pl.ds(half * H, H)], ref.at[:, pl.ds(half * H, H)], out_sem.at[t_out]
            )
            o.start()
            outs.append(o)
            t_out += 1

    each(lambda d: giveback(d).wait_send())
    for arm in range(2):
        for d in range(1, 5):
            for m in range(2):
                if ag_has(arm, d, m):
                    ag(arm, d, m).wait_send()
                    for half in range(2):
                        rs_copy(arm, d, m, half).wait_send()
    for o in outs:
        o.wait()


def local(tokens, routes, scores, out_grad, w_up, w_down):
    n_dp, n_ex = lax.axis_size("dp"), lax.axis_size("expert")
    T, D = tokens.shape
    FB = w_up.shape[1]
    S = n_ex * ROWS
    F = n_dp * FB
    any_spec = pl.BlockSpec(memory_space=pl.ANY)
    vmem_spec = pl.BlockSpec(memory_space=pltpu.VMEM)
    dma = pltpu.SemaphoreType.DMA
    gt, gs, gu, gd = pl.pallas_call(
        functools.partial(kernel, n_dp, n_ex, D, FB, T),
        out_shape=[
            jax.ShapeDtypeStruct((T, D), BF),
            jax.ShapeDtypeStruct((T, 2), BF),
            jax.ShapeDtypeStruct((FB, D), BF),
            jax.ShapeDtypeStruct((FB, D), BF),
        ],
        in_specs=[any_spec] * 4 + [vmem_spec] * 2,
        out_specs=[any_spec, vmem_spec, any_spec, any_spec],
        scratch_shapes=[
            pltpu.VMEM((T, D), BF),
            pltpu.VMEM((T, D), BF),
            pltpu.VMEM((S, 2 * D + LANES), BF),
            pltpu.VMEM((S, 2 * D + LANES), BF),
            pltpu.VMEM((S, D + LANES), BF),
            pltpu.VMEM((F, D), BF),
            pltpu.VMEM((F, D), BF),
            pltpu.VMEM((2, 4, 2, FB, D), BF),
            pltpu.VMEM((2, FB, D), BF),
            pltpu.VMEM((S, F), BF),
            pltpu.VMEM((F, S), BF),
            pltpu.VMEM((F, S), BF),
            pltpu.VMEM((S, LANES), F32),
            pltpu.VMEM((2, T, S), BF),
            dma((4,)),
            dma((2, 4, 2)),
            dma((2, 4, 2)),
            dma((n_ex,)),
            dma((n_ex,)),
            dma((n_ex,)),
            dma((n_ex,)),
            dma((2, 4, 2, 2)),
            dma((2, 4, 2, 2)),
            dma((2, 2)),
            dma((5,)),
        ],
        compiler_params=pltpu.CompilerParams(
            collective_id=0, has_side_effects=True, vmem_limit_bytes=62 * 2**20
        ),
    )(tokens, out_grad, w_up[0], w_down[0], routes, scores)
    return gt, gs, gu[None], gd[None]


def solution(mesh):
    rows = P(("dp", "expert"), None)
    weights = P("expert", "dp", None)
    return jax.shard_map(
        local,
        mesh=mesh,
        in_specs=(rows, rows, rows, rows, weights, weights),
        out_specs=(rows, rows, weights, weights),
        check_vma=False,
    )
```

```python
import functools

import jax
import jax.numpy as jnp
from jax import lax
from jax.experimental import pallas as pl
from jax.experimental.pallas import tpu as pltpu
from jax.sharding import PartitionSpec as P

MESH = pl.DeviceIdType.MESH
BF = jnp.bfloat16
F32 = jnp.float32
ROWS = 16
LANES = 128


def dot_nn(a, b):
    return lax.dot_general(a, b, (((1,), (0,)), ((), ())), preferred_element_type=F32)


def dot_nt(a, b):
    return lax.dot_general(a, b, (((1,), (1,)), ((), ())), preferred_element_type=F32)


def negative(d):
    return ((4 - d // 8) % 4) * 8 + ((4 - (d // 2) % 4) % 4) * 2 + d % 2


def send_order():
    def hops(d):
        x, y = d // 8, (d // 2) % 4
        return min(x, 4 - x) + min(y, 4 - y)

    pairs = []
    for d in sorted(range(1, 32), key=lambda d: -hops(d)):
        for e in (d, negative(d)):
            if e not in pairs:
                pairs.append(e)
    mixed = []
    while pairs:
        mixed.append(pairs.pop(0))
        if pairs:
            mixed.append(pairs.pop())
    return mixed


def kernel(
    n_dp, n_ex, D, FB, T,
    tok_ref, grad_ref, up_ref, down_ref, routes_ref, scores_ref,
    gtok_ref, gscore_ref, gup_ref, gdown_ref,
    tokv, gradv, send, recv, back, wup, wdn, rs, far, du, dut, ht, sacc, pmat, ptt,
    loc_sem, ag_s, ag_r, di_s, di_r, re_s, re_r, rs_s, rs_r, far_s, out_sem,
):
    g = lax.axis_index("dp")
    me = lax.axis_index("expert")
    right, left = lax.rem(g + 1, n_dp), lax.rem(g + n_dp - 1, n_dp)
    S = n_ex * ROWS
    H = D // 2
    mx, my, mc = me // 8, (me // 2) % 4, me % 2

    def peer(d, sign):
        px = (mx + sign * (d // 8) + 4) % 4
        py = (my + sign * ((d // 2) % 4) + 4) % 4
        return px * 8 + py * 2 + (mc + d) % 2

    loads = [
        pltpu.make_async_copy(tok_ref, tokv, loc_sem.at[0]),
        pltpu.make_async_copy(grad_ref, gradv, loc_sem.at[1]),
        pltpu.make_async_copy(up_ref, wup.at[pl.ds(0, FB)], loc_sem.at[2]),
        pltpu.make_async_copy(down_ref, wdn.at[pl.ds(0, FB)], loc_sem.at[3]),
    ]
    for c in loads:
        c.start()

    barrier = pltpu.get_barrier_semaphore()
    for z in (right, left):
        pl.semaphore_signal(barrier, inc=1, device_id=(z, me), device_id_type=MESH)

    def greet(d, _):
        pl.semaphore_signal(
            barrier, inc=1, device_id=(g, peer(d, 1)), device_id_type=MESH
        )
        return 0

    lax.fori_loop(1, n_ex, greet, 0)
    pl.semaphore_wait(barrier, n_ex + 1)

    def slot(arm, d):
        return 0 if d == 0 else (7 if d == 4 else 2 * d - 1 + arm)

    def ag(arm, d, m):
        buf, own = (wup, up_ref) if m == 0 else (wdn, down_ref)
        src = own if d == 1 else buf.at[pl.ds(slot(arm, d - 1) * FB, FB)]
        return pltpu.make_async_remote_copy(
            src_ref=src,
            dst_ref=buf.at[pl.ds(slot(arm, d) * FB, FB)],
            send_sem=ag_s.at[arm, d - 1, m],
            recv_sem=ag_r.at[arm, d - 1, m],
            device_id=(right if arm == 0 else left, me),
            device_id_type=MESH,
        )

    def ag_has(arm, d, m):
        return d <= 3 or m == arm

    def order(arm):
        return (0, 1) if arm == 0 else (1, 0)

    for i in range(2):
        for arm in range(2):
            ag(arm, 1, order(arm)[i]).start()

    def ag_step(d):
        for i in range(2):
            for arm in range(2):
                m = order(arm)[i]
                if ag_has(arm, d, m):
                    ag(arm, d, m).wait_recv()
                    if d < 4 and ag_has(arm, d + 1, m):
                        ag(arm, d + 1, m).start()

    expert = lax.broadcasted_iota(jnp.int32, (n_ex, T), 0)
    rels, onehots = [], []
    for k in range(2):
        to = routes_ref[k : k + 1, :]
        rx = ((to >> 3) - mx + 4) & 3
        ry = (((to >> 1) & 3) - my + 4) & 3
        rel = rx * 8 + ry * 2 + (((to & 1) + mc) & 1)
        rels.append(rel)
        onehots.append((expert == rel).astype(F32))
    tri = (
        lax.broadcasted_iota(jnp.int32, (T, T), 0) < lax.broadcasted_iota(jnp.int32, (T, T), 1)
    ).astype(F32)
    before = dot_nn((onehots[0] + onehots[1]).astype(BF), tri.astype(BF))
    slots = lax.broadcasted_iota(jnp.int32, (S, T), 0)
    score = jnp.zeros((S, 1), F32)
    pt = jnp.zeros((S, T), F32)
    for k in range(2):
        rank = jnp.sum(before * onehots[k], axis=0, keepdims=True).astype(jnp.int32)
        place = (slots == rels[k] * ROWS + rank).astype(F32)
        pmat[k] = place.astype(BF)
        score += jnp.sum(place * scores_ref[k : k + 1, :].astype(F32), axis=1, keepdims=True)
        pt += place
    ptt[...] = pt.T.astype(BF)
    pt = pt.astype(BF)
    cols = D // 7
    loads[0].wait()
    for j in range(7):
        send[:, j * cols : (j + 1) * cols] = dot_nn(pt, tokv[:, j * cols : (j + 1) * cols]).astype(BF)
    loads[1].wait()
    for j in range(7):
        send[:, D + j * cols : D + (j + 1) * cols] = dot_nn(
            pt, gradv[:, j * cols : (j + 1) * cols]
        ).astype(BF)
    send[:, 2 * D :] = jnp.broadcast_to(score, (S, LANES)).astype(BF)
    recv[0:ROWS, :] = send[0:ROWS, :]

    def block(d):
        return pl.ds(pl.multiple_of(d * ROWS, ROWS), ROWS)

    def dispatch(d):
        return pltpu.make_async_remote_copy(
            src_ref=send.at[block(d)],
            dst_ref=recv.at[block(d)],
            send_sem=di_s.at[d],
            recv_sem=di_r.at[d],
            device_id=(g, peer(d, 1)),
            device_id_type=MESH,
        )

    def giveback(d):
        return pltpu.make_async_remote_copy(
            src_ref=send.at[block(d), pl.ds(0, D + LANES)],
            dst_ref=back.at[block(d)],
            send_sem=re_s.at[d],
            recv_sem=re_r.at[d],
            device_id=(g, peer(d, -1)),
            device_id_type=MESH,
        )

    def each(action):
        def body(d, _):
            action(d)
            return 0

        lax.fori_loop(1, n_ex, body, 0)

    for d in send_order():
        dispatch(jnp.where(mc == 0, d, negative(d))).start()
    sacc[...] = jnp.zeros_like(sacc)

    def hidden(first, count):
        n = count * FB
        rows = slice(first * FB, first * FB + n)
        c = recv[:, 2 * D :].astype(F32)
        if count == 2:
            c = jnp.concatenate([c, c], axis=1)
        u = dot_nt(recv[:, :D], wup[rows, :])
        s = dot_nt(recv[:, D : 2 * D], wdn[rows, :])
        sig = jax.nn.sigmoid(u)
        h = (u * sig).astype(BF).astype(F32)
        score = h * s
        for i in range(count):
            sacc[...] += score[:, i * FB : (i + 1) * FB]
        dpre = c * s * (sig * (1.0 + u * (1.0 - sig)))
        du[:, rows] = dpre.astype(BF)
        dut[rows, :] = dpre.T.astype(BF)
        ht[rows, :] = (h * c).T.astype(BF)

    ag_step(1)
    ag_step(2)
    ag_step(3)
    each(lambda d: dispatch(d).wait_recv())
    for c in loads[2:]:
        c.wait()
    hidden(0, 1)
    for d in (1, 2, 3):
        hidden(2 * d - 1, 2)
    ag_step(4)
    hidden(7, 1)

    def term(chunk, m, half):
        lhs = dut if m == 0 else ht
        at = (0 if m == 0 else D) + half * H
        return dot_nn(lhs[chunk * FB : (chunk + 1) * FB, :], recv[:, at : at + H])

    def rs_copy(arm, d, m, half):
        cs = pl.ds(half * H, H)
        src = far.at[arm, :, cs] if d == 4 else rs.at[arm, d, m, :, cs]
        return pltpu.make_async_remote_copy(
            src_ref=src,
            dst_ref=rs.at[arm, d - 1, m, :, cs],
            send_sem=far_s.at[arm, half] if d == 4 else rs_s.at[arm, d, m, half],
            recv_sem=rs_r.at[arm, d - 1, m, half],
            device_id=(left if arm == 0 else right, me),
            device_id_type=MESH,
        )

    def rs_piece(arm, d, m, half):
        cs = slice(half * H, (half + 1) * H)
        t = term(slot(arm, d), m, half)
        if d == 4:
            far[arm, :, cs] = t.astype(BF)
        elif d == 3 and m != arm:
            rs[arm, d, m, :, cs] = t.astype(BF)
        else:
            rs_copy(arm, d + 1, m, half).wait_recv()
            rs[arm, d, m, :, cs] = (t + rs[arm, d, m, :, cs].astype(F32)).astype(BF)
        rs_copy(arm, d, m, half).start()

    for half in range(2):
        for arm in range(2):
            rs_piece(arm, 4, arm, half)
    for half in range(2):
        for arm in range(2):
            rs_piece(arm, 3, 1 - arm, half)

    each(lambda d: dispatch(d).wait_send())
    for j in range(7):
        send[:, j * cols : (j + 1) * cols] = dot_nn(
            du[...], wup[:, j * cols : (j + 1) * cols]
        ).astype(BF)
    total = jnp.sum(sacc[...], axis=1, keepdims=True)
    send[:, D : D + LANES] = jnp.broadcast_to(total, (S, LANES)).astype(BF)
    back[0:ROWS, :] = send[0:ROWS, 0 : D + LANES]
    for d in send_order():
        giveback(jnp.where(mc == 0, d, negative(d))).start()

    for half in range(2):
        for arm in range(2):
            rs_piece(arm, 3, arm, half)
    for d in (2, 1):
        for i in range(2):
            for half in range(2):
                for arm in range(2):
                    rs_piece(arm, d, (1 - arm) if i == 0 else arm, half)

    each(lambda d: giveback(d).wait_recv())
    for j in range(7):
        tokv[:, j * cols : (j + 1) * cols] = dot_nn(ptt[...], back[:, j * cols : (j + 1) * cols]).astype(BF)
    outs = [pltpu.make_async_copy(tokv, gtok_ref, out_sem.at[0])]
    outs[0].start()
    given = back[:, D:].astype(F32)
    for k in range(2):
        gscore_ref[k : k + 1, :] = jnp.sum(pmat[k].astype(F32) * given, axis=0, keepdims=True).astype(BF)

    t_out = 1
    for half in range(2):
        for m in range(2):
            cs = slice(half * H, (half + 1) * H)
            t = term(0, m, half)
            for arm in range(2):
                rs_copy(arm, 1, m, half).wait_recv()
                t = t + rs[arm, 0, m, :, cs].astype(F32)
            rs[0, 0, m, :, cs] = t.astype(BF)
            ref = gup_ref if m == 0 else gdown_ref
            o = pltpu.make_async_copy(
                rs.at[0, 0, m, :, pl.ds(half * H, H)], ref.at[:, pl.ds(half * H, H)], out_sem.at[t_out]
            )
            o.start()
            outs.append(o)
            t_out += 1

    each(lambda d: giveback(d).wait_send())
    for arm in range(2):
        for d in range(1, 5):
            for m in range(2):
                if ag_has(arm, d, m):
                    ag(arm, d, m).wait_send()
                    for half in range(2):
                        rs_copy(arm, d, m, half).wait_send()
    for o in outs:
        o.wait()


def local(tokens, routes, scores, out_grad, w_up, w_down):
    n_dp, n_ex = lax.axis_size("dp"), lax.axis_size("expert")
    T, D = tokens.shape
    FB = w_up.shape[1]
    S = n_ex * ROWS
    F = n_dp * FB
    any_spec = pl.BlockSpec(memory_space=pl.ANY)
    vmem_spec = pl.BlockSpec(memory_space=pltpu.VMEM)
    dma = pltpu.SemaphoreType.DMA
    gt, gs, gu, gd = pl.pallas_call(
        functools.partial(kernel, n_dp, n_ex, D, FB, T),
        out_shape=[
            jax.ShapeDtypeStruct((T, D), BF),
            jax.ShapeDtypeStruct((2, T), BF),
            jax.ShapeDtypeStruct((FB, D), BF),
            jax.ShapeDtypeStruct((FB, D), BF),
        ],
        in_specs=[any_spec] * 4 + [vmem_spec] * 2,
        out_specs=[any_spec, vmem_spec, any_spec, any_spec],
        scratch_shapes=[
            pltpu.VMEM((T, D), BF),
            pltpu.VMEM((T, D), BF),
            pltpu.VMEM((S, 2 * D + LANES), BF),
            pltpu.VMEM((S, 2 * D + LANES), BF),
            pltpu.VMEM((S, D + LANES), BF),
            pltpu.VMEM((F, D), BF),
            pltpu.VMEM((F, D), BF),
            pltpu.VMEM((2, 4, 2, FB, D), BF),
            pltpu.VMEM((2, FB, D), BF),
            pltpu.VMEM((S, F), BF),
            pltpu.VMEM((F, S), BF),
            pltpu.VMEM((F, S), BF),
            pltpu.VMEM((S, LANES), F32),
            pltpu.VMEM((2, S, T), BF),
            pltpu.VMEM((T, S), BF),
            dma((4,)),
            dma((2, 4, 2)),
            dma((2, 4, 2)),
            dma((n_ex,)),
            dma((n_ex,)),
            dma((n_ex,)),
            dma((n_ex,)),
            dma((2, 4, 2, 2)),
            dma((2, 4, 2, 2)),
            dma((2, 2)),
            dma((5,)),
        ],
        compiler_params=pltpu.CompilerParams(
            collective_id=0, has_side_effects=True, vmem_limit_bytes=62 * 2**20
        ),
    )(tokens, out_grad, w_up[0], w_down[0], routes.T, scores.T)
    return gt, gs.T, gu[None], gd[None]


def solution(mesh):
    rows = P(("dp", "expert"), None)
    weights = P("expert", "dp", None)
    return jax.shard_map(
        local,
        mesh=mesh,
        in_specs=(rows, rows, rows, rows, weights, weights),
        out_specs=(rows, rows, weights, weights),
        check_vma=False,
    )
```

```python
import functools

import jax
import jax.numpy as jnp
from jax import lax
from jax.experimental import pallas as pl
from jax.experimental.pallas import tpu as pltpu
from jax.sharding import PartitionSpec as P

MESH = pl.DeviceIdType.MESH
BF = jnp.bfloat16
F32 = jnp.float32
ROWS = 16
LANES = 128


def dot_nn(a, b):
    return lax.dot_general(a, b, (((1,), (0,)), ((), ())), preferred_element_type=F32)


def dot_nt(a, b):
    return lax.dot_general(a, b, (((1,), (1,)), ((), ())), preferred_element_type=F32)


def negative(d):
    return ((4 - d // 8) % 4) * 8 + ((4 - (d // 2) % 4) % 4) * 2 + d % 2


def send_order():
    def hops(d):
        x, y = d // 8, (d // 2) % 4
        return min(x, 4 - x) + min(y, 4 - y)

    pairs = []
    for d in sorted(range(1, 32), key=lambda d: -hops(d)):
        for e in (d, negative(d)):
            if e not in pairs:
                pairs.append(e)
    mixed = []
    while pairs:
        mixed.append(pairs.pop(0))
        if pairs:
            mixed.append(pairs.pop())
    return mixed


def kernel(
    n_dp, n_ex, D, FB, T,
    tok_ref, grad_ref, up_ref, down_ref, routes_ref, scores_ref,
    gtok_ref, gscore_ref, near_ref, late_ref,
    tokv, gradv, send, recv, back, wup, wdn, rs, far, du, dut, ht, sacc, pmat, ptt,
    loc_sem, ag_s, ag_r, di_s, di_r, re_s, re_r, rs_s, rs_r, far_s, out_sem,
):
    g = lax.axis_index("dp")
    me = lax.axis_index("expert")
    right, left = lax.rem(g + 1, n_dp), lax.rem(g + n_dp - 1, n_dp)
    S = n_ex * ROWS
    H = D // 2
    mx, my, mc = me // 8, (me // 2) % 4, me % 2

    def peer(d, sign):
        px = (mx + sign * (d // 8) + 4) % 4
        py = (my + sign * ((d // 2) % 4) + 4) % 4
        return px * 8 + py * 2 + (mc + d) % 2

    loads = [
        pltpu.make_async_copy(tok_ref, tokv, loc_sem.at[0]),
        pltpu.make_async_copy(grad_ref, gradv, loc_sem.at[1]),
        pltpu.make_async_copy(up_ref, wup.at[pl.ds(0, FB)], loc_sem.at[2]),
        pltpu.make_async_copy(down_ref, wdn.at[pl.ds(0, FB)], loc_sem.at[3]),
    ]
    for c in loads:
        c.start()

    barrier = pltpu.get_barrier_semaphore()
    for z in (right, left):
        pl.semaphore_signal(barrier, inc=1, device_id=(z, me), device_id_type=MESH)

    def greet(d, _):
        pl.semaphore_signal(
            barrier, inc=1, device_id=(g, peer(d, 1)), device_id_type=MESH
        )
        return 0

    lax.fori_loop(1, n_ex, greet, 0)
    pl.semaphore_wait(barrier, n_ex + 1)

    def slot(arm, d):
        return 0 if d == 0 else (7 if d == 4 else 2 * d - 1 + arm)

    def ag(arm, d, m):
        buf, own = (wup, up_ref) if m == 0 else (wdn, down_ref)
        src = own if d == 1 else buf.at[pl.ds(slot(arm, d - 1) * FB, FB)]
        return pltpu.make_async_remote_copy(
            src_ref=src,
            dst_ref=buf.at[pl.ds(slot(arm, d) * FB, FB)],
            send_sem=ag_s.at[arm, d - 1, m],
            recv_sem=ag_r.at[arm, d - 1, m],
            device_id=(right if arm == 0 else left, me),
            device_id_type=MESH,
        )

    def ag_has(arm, d, m):
        return d <= 3 or m == arm

    def order(arm):
        return (0, 1) if arm == 0 else (1, 0)

    for i in range(2):
        for arm in range(2):
            ag(arm, 1, order(arm)[i]).start()

    def ag_step(d):
        for i in range(2):
            for arm in range(2):
                m = order(arm)[i]
                if ag_has(arm, d, m):
                    ag(arm, d, m).wait_recv()
                    if d < 4 and ag_has(arm, d + 1, m):
                        ag(arm, d + 1, m).start()

    expert = lax.broadcasted_iota(jnp.int32, (n_ex, T), 0)
    rels, onehots = [], []
    for k in range(2):
        to = routes_ref[k : k + 1, :]
        rx = ((to >> 3) - mx + 4) & 3
        ry = (((to >> 1) & 3) - my + 4) & 3
        rel = rx * 8 + ry * 2 + (((to & 1) + mc) & 1)
        rels.append(rel)
        onehots.append((expert == rel).astype(F32))
    tri = (
        lax.broadcasted_iota(jnp.int32, (T, T), 0) < lax.broadcasted_iota(jnp.int32, (T, T), 1)
    ).astype(F32)
    before = dot_nn((onehots[0] + onehots[1]).astype(BF), tri.astype(BF))
    slots = lax.broadcasted_iota(jnp.int32, (S, T), 0)
    score = jnp.zeros((S, 1), F32)
    pt = jnp.zeros((S, T), F32)
    for k in range(2):
        rank = jnp.sum(before * onehots[k], axis=0, keepdims=True).astype(jnp.int32)
        place = (slots == rels[k] * ROWS + rank).astype(F32)
        pmat[k] = place.astype(BF)
        score += jnp.sum(place * scores_ref[k : k + 1, :].astype(F32), axis=1, keepdims=True)
        pt += place
    ptt[...] = pt.T.astype(BF)
    pt = pt.astype(BF)
    cols = D // 7
    loads[0].wait()
    for j in range(7):
        send[:, j * cols : (j + 1) * cols] = dot_nn(pt, tokv[:, j * cols : (j + 1) * cols]).astype(BF)
    loads[1].wait()
    for j in range(7):
        send[:, D + j * cols : D + (j + 1) * cols] = dot_nn(
            pt, gradv[:, j * cols : (j + 1) * cols]
        ).astype(BF)
    send[:, 2 * D :] = jnp.broadcast_to(score, (S, LANES)).astype(BF)
    recv[0:ROWS, :] = send[0:ROWS, :]

    def block(d):
        return pl.ds(pl.multiple_of(d * ROWS, ROWS), ROWS)

    def dispatch(d):
        return pltpu.make_async_remote_copy(
            src_ref=send.at[block(d)],
            dst_ref=recv.at[block(d)],
            send_sem=di_s.at[d],
            recv_sem=di_r.at[d],
            device_id=(g, peer(d, 1)),
            device_id_type=MESH,
        )

    def giveback(d):
        return pltpu.make_async_remote_copy(
            src_ref=send.at[block(d), pl.ds(0, D + LANES)],
            dst_ref=back.at[block(d)],
            send_sem=re_s.at[d],
            recv_sem=re_r.at[d],
            device_id=(g, peer(d, -1)),
            device_id_type=MESH,
        )

    def each(action):
        def body(d, _):
            action(d)
            return 0

        lax.fori_loop(1, n_ex, body, 0)

    for d in send_order():
        dispatch(jnp.where(mc == 0, d, negative(d))).start()
    sacc[...] = jnp.zeros_like(sacc)

    def hidden(first, count):
        n = count * FB
        rows = slice(first * FB, first * FB + n)
        c = recv[:, 2 * D :].astype(F32)
        if count == 2:
            c = jnp.concatenate([c, c], axis=1)
        u = dot_nt(recv[:, :D], wup[rows, :])
        s = dot_nt(recv[:, D : 2 * D], wdn[rows, :])
        sig = jax.nn.sigmoid(u)
        h = (u * sig).astype(BF).astype(F32)
        score = h * s
        for i in range(count):
            sacc[...] += score[:, i * FB : (i + 1) * FB]
        dpre = c * s * (sig * (1.0 + u * (1.0 - sig)))
        du[:, rows] = dpre.astype(BF)
        dut[rows, :] = dpre.T.astype(BF)
        ht[rows, :] = (h * c).T.astype(BF)

    ag_step(1)
    ag_step(2)
    each(lambda d: dispatch(d).wait_recv())
    for c in loads[2:]:
        c.wait()
    hidden(0, 1)
    hidden(1, 2)
    hidden(3, 2)
    ag_step(3)
    hidden(5, 2)

    def term(chunk, m, half):
        lhs = dut if m == 0 else ht
        at = (0 if m == 0 else D) + half * H
        return dot_nn(lhs[chunk * FB : (chunk + 1) * FB, :], recv[:, at : at + H])

    def rs_copy(arm, d, m, half):
        cs = pl.ds(half * H, H)
        src = far.at[arm, :, cs] if d == 4 else rs.at[arm, d, m, :, cs]
        return pltpu.make_async_remote_copy(
            src_ref=src,
            dst_ref=late_ref.at[m, :, cs] if d == 1 and m == arm else rs.at[arm, d - 1, m, :, cs],
            send_sem=far_s.at[arm, half] if d == 4 else rs_s.at[arm, d, m, half],
            recv_sem=rs_r.at[arm, d - 1, m, half],
            device_id=(left if arm == 0 else right, me),
            device_id_type=MESH,
        )

    def rs_piece(arm, d, m, half):
        cs = slice(half * H, (half + 1) * H)
        t = term(slot(arm, d), m, half)
        if d == 4:
            far[arm, :, cs] = t.astype(BF)
        elif d == 3 and m != arm:
            rs[arm, d, m, :, cs] = t.astype(BF)
        else:
            rs_copy(arm, d + 1, m, half).wait_recv()
            rs[arm, d, m, :, cs] = (t + rs[arm, d, m, :, cs].astype(F32)).astype(BF)
        rs_copy(arm, d, m, half).start()

    for half in range(2):
        for arm in range(2):
            rs_piece(arm, 3, 1 - arm, half)
    ag_step(4)
    hidden(7, 1)
    for half in range(2):
        for arm in range(2):
            rs_piece(arm, 4, arm, half)

    each(lambda d: dispatch(d).wait_send())
    for j in range(7):
        send[:, j * cols : (j + 1) * cols] = dot_nn(
            du[...], wup[:, j * cols : (j + 1) * cols]
        ).astype(BF)
    total = jnp.sum(sacc[...], axis=1, keepdims=True)
    send[:, D : D + LANES] = jnp.broadcast_to(total, (S, LANES)).astype(BF)
    back[0:ROWS, :] = send[0:ROWS, 0 : D + LANES]
    for d in send_order():
        giveback(jnp.where(mc == 0, d, negative(d))).start()

    for half in range(2):
        for arm in range(2):
            rs_piece(arm, 3, arm, half)
    for d in (2, 1):
        for i in range(2):
            for half in range(2):
                for arm in range(2):
                    rs_piece(arm, d, (1 - arm) if i == 0 else arm, half)

    each(lambda d: giveback(d).wait_recv())
    for j in range(7):
        tokv[:, j * cols : (j + 1) * cols] = dot_nn(ptt[...], back[:, j * cols : (j + 1) * cols]).astype(BF)
    outs = [pltpu.make_async_copy(tokv, gtok_ref, out_sem.at[0])]
    outs[0].start()
    given = back[:, D:].astype(F32)
    for k in range(2):
        gscore_ref[k : k + 1, :] = jnp.sum(pmat[k].astype(F32) * given, axis=0, keepdims=True).astype(BF)

    for m in range(2):
        for half in range(2):
            cs = slice(half * H, (half + 1) * H)
            t = term(0, m, half)
            rs_copy(1 - m, 1, m, half).wait_recv()
            rs[1 - m, 0, m, :, cs] = (t + rs[1 - m, 0, m, :, cs].astype(F32)).astype(BF)
        outs.append(pltpu.make_async_copy(rs.at[1 - m, 0, m], near_ref.at[m], out_sem.at[1 + m]))
        outs[-1].start()
    each(lambda d: giveback(d).wait_send())
    for arm in range(2):
        for d in range(1, 5):
            for m in range(2):
                if ag_has(arm, d, m):
                    ag(arm, d, m).wait_send()
                    for half in range(2):
                        rs_copy(arm, d, m, half).wait_send()
    for o in outs:
        o.wait()
    for half in range(2):
        for m in range(2):
            rs_copy(m, 1, m, half).wait_recv()


def local(tokens, routes, scores, out_grad, w_up, w_down):
    n_dp, n_ex = lax.axis_size("dp"), lax.axis_size("expert")
    T, D = tokens.shape
    FB = w_up.shape[1]
    S = n_ex * ROWS
    F = n_dp * FB
    any_spec = pl.BlockSpec(memory_space=pl.ANY)
    vmem_spec = pl.BlockSpec(memory_space=pltpu.VMEM)
    dma = pltpu.SemaphoreType.DMA
    gt, gs, near, late = pl.pallas_call(
        functools.partial(kernel, n_dp, n_ex, D, FB, T),
        out_shape=[
            jax.ShapeDtypeStruct((T, D), BF),
            jax.ShapeDtypeStruct((2, T), BF),
            jax.ShapeDtypeStruct((2, FB, D), BF),
            jax.ShapeDtypeStruct((2, FB, D), BF),
        ],
        in_specs=[any_spec] * 4 + [vmem_spec] * 2,
        out_specs=[any_spec, vmem_spec, any_spec, any_spec],
        scratch_shapes=[
            pltpu.VMEM((T, D), BF),
            pltpu.VMEM((T, D), BF),
            pltpu.VMEM((S, 2 * D + LANES), BF),
            pltpu.VMEM((S, 2 * D + LANES), BF),
            pltpu.VMEM((S, D + LANES), BF),
            pltpu.VMEM((F, D), BF),
            pltpu.VMEM((F, D), BF),
            pltpu.VMEM((2, 4, 2, FB, D), BF),
            pltpu.VMEM((2, FB, D), BF),
            pltpu.VMEM((S, F), BF),
            pltpu.VMEM((F, S), BF),
            pltpu.VMEM((F, S), BF),
            pltpu.VMEM((S, LANES), F32),
            pltpu.VMEM((2, S, T), BF),
            pltpu.VMEM((T, S), BF),
            dma((4,)),
            dma((2, 4, 2)),
            dma((2, 4, 2)),
            dma((n_ex,)),
            dma((n_ex,)),
            dma((n_ex,)),
            dma((n_ex,)),
            dma((2, 4, 2, 2)),
            dma((2, 4, 2, 2)),
            dma((2, 2)),
            dma((5,)),
        ],
        compiler_params=pltpu.CompilerParams(
            collective_id=0, has_side_effects=True, vmem_limit_bytes=62 * 2**20
        ),
    )(tokens, out_grad, w_up[0], w_down[0], routes.T, scores.T)
    gu, gd = ((near[m].astype(F32) + late[m].astype(F32)).astype(BF) for m in range(2))
    return gt, gs.T, gu[None], gd[None]


def solution(mesh):
    rows = P(("dp", "expert"), None)
    weights = P("expert", "dp", None)
    return jax.shard_map(
        local,
        mesh=mesh,
        in_specs=(rows, rows, rows, rows, weights, weights),
        out_specs=(rows, rows, weights, weights),
        check_vma=False,
    )
```

```python
import functools

import jax
import jax.numpy as jnp
from jax import lax
from jax.experimental import pallas as pl
from jax.experimental.pallas import tpu as pltpu
from jax.sharding import PartitionSpec as P

MESH = pl.DeviceIdType.MESH
BF = jnp.bfloat16
F32 = jnp.float32
ROWS = 16
LANES = 128


def dot_nn(a, b):
    return lax.dot_general(a, b, (((1,), (0,)), ((), ())), preferred_element_type=F32)


def dot_nt(a, b):
    return lax.dot_general(a, b, (((1,), (1,)), ((), ())), preferred_element_type=F32)


def negative(d):
    return ((4 - d // 8) % 4) * 8 + ((4 - (d // 2) % 4) % 4) * 2 + d % 2


def send_order():
    def hops(d):
        x, y = d // 8, (d // 2) % 4
        return min(x, 4 - x) + min(y, 4 - y)

    pairs = []
    for d in sorted(range(1, 32), key=lambda d: -hops(d)):
        for e in (d, negative(d)):
            if e not in pairs:
                pairs.append(e)
    mixed = []
    while pairs:
        mixed.append(pairs.pop(0))
        if pairs:
            mixed.append(pairs.pop())
    return mixed


def kernel(
    n_dp, n_ex, D, FB, T,
    tok_ref, grad_ref, up_ref, down_ref, routes_ref, scores_ref,
    gtok_ref, gscore_ref, near_up, near_down, late_up, late_down,
    tokv, gradv, send, recv, back, wup, wdn, rs, far, du, dut, ht, sacc, pmat, ptt,
    loc_sem, ag_s, ag_r, di_s, di_r, re_s, re_r, rs_s, rs_r, far_s, out_sem,
):
    g = lax.axis_index("dp")
    me = lax.axis_index("expert")
    right, left = lax.rem(g + 1, n_dp), lax.rem(g + n_dp - 1, n_dp)
    S = n_ex * ROWS
    H = D // 2
    mx, my, mc = me // 8, (me // 2) % 4, me % 2

    def peer(d, sign):
        px = (mx + sign * (d // 8) + 4) % 4
        py = (my + sign * ((d // 2) % 4) + 4) % 4
        return px * 8 + py * 2 + (mc + d) % 2

    loads = [
        pltpu.make_async_copy(tok_ref, tokv, loc_sem.at[0]),
        pltpu.make_async_copy(grad_ref, gradv, loc_sem.at[1]),
        pltpu.make_async_copy(up_ref, wup.at[pl.ds(0, FB)], loc_sem.at[2]),
        pltpu.make_async_copy(down_ref, wdn.at[pl.ds(0, FB)], loc_sem.at[3]),
    ]
    for c in loads:
        c.start()

    barrier = pltpu.get_barrier_semaphore()
    for z in (right, left):
        pl.semaphore_signal(barrier, inc=1, device_id=(z, me), device_id_type=MESH)

    def greet(d, _):
        pl.semaphore_signal(
            barrier, inc=1, device_id=(g, peer(d, 1)), device_id_type=MESH
        )
        return 0

    lax.fori_loop(1, n_ex, greet, 0)
    pl.semaphore_wait(barrier, n_ex + 1)

    def slot(arm, d):
        return 0 if d == 0 else (7 if d == 4 else 2 * d - 1 + arm)

    def ag(arm, d, m):
        buf, own = (wup, up_ref) if m == 0 else (wdn, down_ref)
        src = own if d == 1 else buf.at[pl.ds(slot(arm, d - 1) * FB, FB)]
        return pltpu.make_async_remote_copy(
            src_ref=src,
            dst_ref=buf.at[pl.ds(slot(arm, d) * FB, FB)],
            send_sem=ag_s.at[arm, d - 1, m],
            recv_sem=ag_r.at[arm, d - 1, m],
            device_id=(right if arm == 0 else left, me),
            device_id_type=MESH,
        )

    def ag_has(arm, d, m):
        return d <= 3 or m == arm

    def order(arm):
        return (0, 1) if arm == 0 else (1, 0)

    for i in range(2):
        for arm in range(2):
            ag(arm, 1, order(arm)[i]).start()

    def ag_step(d):
        for i in range(2):
            for arm in range(2):
                m = order(arm)[i]
                if ag_has(arm, d, m):
                    ag(arm, d, m).wait_recv()
                    if d < 4 and ag_has(arm, d + 1, m):
                        ag(arm, d + 1, m).start()

    expert = lax.broadcasted_iota(jnp.int32, (n_ex, T), 0)
    rels, onehots = [], []
    for k in range(2):
        to = routes_ref[k : k + 1, :]
        rx = ((to >> 3) - mx + 4) & 3
        ry = (((to >> 1) & 3) - my + 4) & 3
        rel = rx * 8 + ry * 2 + (((to & 1) + mc) & 1)
        rels.append(rel)
        onehots.append((expert == rel).astype(F32))
    tri = (
        lax.broadcasted_iota(jnp.int32, (T, T), 0) < lax.broadcasted_iota(jnp.int32, (T, T), 1)
    ).astype(F32)
    before = dot_nn((onehots[0] + onehots[1]).astype(BF), tri.astype(BF))
    slots = lax.broadcasted_iota(jnp.int32, (S, T), 0)
    score = jnp.zeros((S, 1), F32)
    pt = jnp.zeros((S, T), F32)
    for k in range(2):
        rank = jnp.sum(before * onehots[k], axis=0, keepdims=True).astype(jnp.int32)
        place = (slots == rels[k] * ROWS + rank).astype(F32)
        pmat[k] = place.astype(BF)
        score += jnp.sum(place * scores_ref[k : k + 1, :].astype(F32), axis=1, keepdims=True)
        pt += place
    ptt[...] = pt.T.astype(BF)
    pt = pt.astype(BF)
    cols = D // 7
    loads[0].wait()
    for j in range(7):
        send[:, j * cols : (j + 1) * cols] = dot_nn(pt, tokv[:, j * cols : (j + 1) * cols]).astype(BF)
    loads[1].wait()
    for j in range(7):
        send[:, D + j * cols : D + (j + 1) * cols] = dot_nn(
            pt, gradv[:, j * cols : (j + 1) * cols]
        ).astype(BF)
    send[:, 2 * D :] = jnp.broadcast_to(score, (S, LANES)).astype(BF)
    recv[0:ROWS, :] = send[0:ROWS, :]

    def block(d):
        return pl.ds(pl.multiple_of(d * ROWS, ROWS), ROWS)

    def dispatch(d):
        return pltpu.make_async_remote_copy(
            src_ref=send.at[block(d)],
            dst_ref=recv.at[block(d)],
            send_sem=di_s.at[d],
            recv_sem=di_r.at[d],
            device_id=(g, peer(d, 1)),
            device_id_type=MESH,
        )

    def giveback(d):
        return pltpu.make_async_remote_copy(
            src_ref=send.at[block(d), pl.ds(0, D + LANES)],
            dst_ref=back.at[block(d)],
            send_sem=re_s.at[d],
            recv_sem=re_r.at[d],
            device_id=(g, peer(d, -1)),
            device_id_type=MESH,
        )

    def each(action):
        def body(d, _):
            action(d)
            return 0

        lax.fori_loop(1, n_ex, body, 0)

    for d in send_order():
        dispatch(jnp.where(mc == 0, d, negative(d))).start()
    sacc[...] = jnp.zeros_like(sacc)

    def hidden(first, count):
        n = count * FB
        rows = slice(first * FB, first * FB + n)
        c = recv[:, 2 * D :].astype(F32)
        if count == 2:
            c = jnp.concatenate([c, c], axis=1)
        u = dot_nt(recv[:, :D], wup[rows, :])
        s = dot_nt(recv[:, D : 2 * D], wdn[rows, :])
        sig = jax.nn.sigmoid(u)
        h = (u * sig).astype(BF).astype(F32)
        score = h * s
        for i in range(count):
            sacc[...] += score[:, i * FB : (i + 1) * FB]
        dpre = c * s * (sig * (1.0 + u * (1.0 - sig)))
        du[:, rows] = dpre.astype(BF)
        dut[rows, :] = dpre.T.astype(BF)
        ht[rows, :] = (h * c).T.astype(BF)

    ag_step(1)
    ag_step(2)
    each(lambda d: dispatch(d).wait_recv())
    for c in loads[2:]:
        c.wait()
    hidden(0, 1)
    hidden(1, 2)
    hidden(3, 2)
    ag_step(3)
    hidden(5, 2)

    def term(chunk, m, half):
        lhs = dut if m == 0 else ht
        at = (0 if m == 0 else D) + half * H
        return dot_nn(lhs[chunk * FB : (chunk + 1) * FB, :], recv[:, at : at + H])

    def rs_copy(arm, d, m, half):
        cs = pl.ds(half * H, H)
        src = far.at[arm, :, cs] if d == 4 else rs.at[arm, d, m, :, cs]
        return pltpu.make_async_remote_copy(
            src_ref=src,
            dst_ref=(late_up, late_down)[m].at[:, cs] if d == 1 and m == arm else rs.at[arm, d - 1, m, :, cs],
            send_sem=far_s.at[arm, half] if d == 4 else rs_s.at[arm, d, m, half],
            recv_sem=rs_r.at[arm, d - 1, m, half],
            device_id=(left if arm == 0 else right, me),
            device_id_type=MESH,
        )

    def rs_piece(arm, d, m, half):
        cs = slice(half * H, (half + 1) * H)
        t = term(slot(arm, d), m, half)
        if d == 4:
            far[arm, :, cs] = t.astype(BF)
        elif d == 3 and m != arm:
            rs[arm, d, m, :, cs] = t.astype(BF)
        else:
            rs_copy(arm, d + 1, m, half).wait_recv()
            rs[arm, d, m, :, cs] = (t + rs[arm, d, m, :, cs].astype(F32)).astype(BF)
        rs_copy(arm, d, m, half).start()

    for half in range(2):
        for arm in range(2):
            rs_piece(arm, 3, 1 - arm, half)
    ag_step(4)
    hidden(7, 1)
    for half in range(2):
        for arm in range(2):
            rs_piece(arm, 4, arm, half)

    each(lambda d: dispatch(d).wait_send())
    for j in range(7):
        send[:, j * cols : (j + 1) * cols] = dot_nn(
            du[...], wup[:, j * cols : (j + 1) * cols]
        ).astype(BF)
    total = jnp.sum(sacc[...], axis=1, keepdims=True)
    send[:, D : D + LANES] = jnp.broadcast_to(total, (S, LANES)).astype(BF)
    back[0:ROWS, :] = send[0:ROWS, 0 : D + LANES]
    for d in send_order():
        giveback(jnp.where(mc == 0, d, negative(d))).start()

    for half in range(2):
        for arm in range(2):
            rs_piece(arm, 3, arm, half)
    for d in (2, 1):
        for i in range(2):
            for half in range(2):
                for arm in range(2):
                    rs_piece(arm, d, (1 - arm) if i == 0 else arm, half)

    each(lambda d: giveback(d).wait_recv())
    for j in range(7):
        tokv[:, j * cols : (j + 1) * cols] = dot_nn(ptt[...], back[:, j * cols : (j + 1) * cols]).astype(BF)
    outs = [pltpu.make_async_copy(tokv, gtok_ref, out_sem.at[0])]
    outs[0].start()
    given = back[:, D:].astype(F32)
    for k in range(2):
        gscore_ref[k : k + 1, :] = jnp.sum(pmat[k].astype(F32) * given, axis=0, keepdims=True).astype(BF)

    for m in range(2):
        for half in range(2):
            cs = slice(half * H, (half + 1) * H)
            t = term(0, m, half)
            rs_copy(1 - m, 1, m, half).wait_recv()
            rs[1 - m, 0, m, :, cs] = (t + rs[1 - m, 0, m, :, cs].astype(F32)).astype(BF)
        outs.append(pltpu.make_async_copy(rs.at[1 - m, 0, m], (near_up, near_down)[m], out_sem.at[1 + m]))
        outs[-1].start()
    each(lambda d: giveback(d).wait_send())
    for arm in range(2):
        for d in range(1, 5):
            for m in range(2):
                if ag_has(arm, d, m):
                    ag(arm, d, m).wait_send()
                    for half in range(2):
                        rs_copy(arm, d, m, half).wait_send()
    for o in outs:
        o.wait()
    for half in range(2):
        for m in range(2):
            rs_copy(m, 1, m, half).wait_recv()


def local(tokens, routes, scores, out_grad, w_up, w_down):
    n_dp, n_ex = lax.axis_size("dp"), lax.axis_size("expert")
    T, D = tokens.shape
    FB = w_up.shape[1]
    S = n_ex * ROWS
    F = n_dp * FB
    any_spec = pl.BlockSpec(memory_space=pl.ANY)
    vmem_spec = pl.BlockSpec(memory_space=pltpu.VMEM)
    dma = pltpu.SemaphoreType.DMA
    gt, gs, *sums = pl.pallas_call(
        functools.partial(kernel, n_dp, n_ex, D, FB, T),
        out_shape=[
            jax.ShapeDtypeStruct((T, D), BF),
            jax.ShapeDtypeStruct((2, T), BF),
            jax.ShapeDtypeStruct((FB, D), BF),
            jax.ShapeDtypeStruct((FB, D), BF),
            jax.ShapeDtypeStruct((FB, D), BF),
            jax.ShapeDtypeStruct((FB, D), BF),
        ],
        in_specs=[any_spec] * 4 + [vmem_spec] * 2,
        out_specs=[any_spec, vmem_spec] + [any_spec] * 4,
        scratch_shapes=[
            pltpu.VMEM((T, D), BF),
            pltpu.VMEM((T, D), BF),
            pltpu.VMEM((S, 2 * D + LANES), BF),
            pltpu.VMEM((S, 2 * D + LANES), BF),
            pltpu.VMEM((S, D + LANES), BF),
            pltpu.VMEM((F, D), BF),
            pltpu.VMEM((F, D), BF),
            pltpu.VMEM((2, 4, 2, FB, D), BF),
            pltpu.VMEM((2, FB, D), BF),
            pltpu.VMEM((S, F), BF),
            pltpu.VMEM((F, S), BF),
            pltpu.VMEM((F, S), BF),
            pltpu.VMEM((S, LANES), F32),
            pltpu.VMEM((2, S, T), BF),
            pltpu.VMEM((T, S), BF),
            dma((4,)),
            dma((2, 4, 2)),
            dma((2, 4, 2)),
            dma((n_ex,)),
            dma((n_ex,)),
            dma((n_ex,)),
            dma((n_ex,)),
            dma((2, 4, 2, 2)),
            dma((2, 4, 2, 2)),
            dma((2, 2)),
            dma((5,)),
        ],
        compiler_params=pltpu.CompilerParams(
            collective_id=0, has_side_effects=True, vmem_limit_bytes=62 * 2**20
        ),
    )(tokens, out_grad, w_up[0], w_down[0], routes.T, scores.T)
    gu, gd = ((sums[m].astype(F32) + sums[2 + m].astype(F32)).astype(BF) for m in range(2))
    return gt, gs.T, gu[None], gd[None]


def solution(mesh):
    rows = P(("dp", "expert"), None)
    weights = P("expert", "dp", None)
    return jax.shard_map(
        local,
        mesh=mesh,
        in_specs=(rows, rows, rows, rows, weights, weights),
        out_specs=(rows, rows, weights, weights),
        check_vma=False,
    )
```
